1024 devices in a mesh: replica: 64 (over z, x_lo, core), tensor: 16 (over y, x_hi).
Axes of the slice: x: 8 (x_hi: 2, x_lo: 4; x = x_hi * 4 + x_lo), y: 8, z: 8, core: 2. Of those that a mesh axis runs over, the one named last changes fastest.
Arguments:
- features: bfloat16 [81920, 5120], P('replica', 'tensor'), may hold values from -6 to 6
- key_grad: bfloat16 [81920, 512], P(('replica', 'tensor')), may hold values from -0.29882812 to 0.29882812
- master: float32 [64, 5120, 512], P('replica', 'tensor'), may hold values from -6 to 6
- exponents: int32 [2], replicated, may hold values from 0 to 5, as said below
Outputs:
- new_master: float32 [64, 5120, 512], P('replica', 'tensor')
- new_working: bfloat16 [64, 5120, 512], P('replica', 'tensor')
- input_grad: bfloat16 [81920, 5120], P('replica', 'tensor')
The draws below stay inside these ranges and needn't reach their ends.
Inputs may be any that keep to these rules, and one draw needn't show every extreme that they name: Two different exponents: one of them is always 5 (the top bit of 64), the other lies in 0 to 4; either may come first.
All inputs are finite; a program needn't handle non-finite values.
Results may differ from the reference program's by a relative error of at most 0.006.
Values may be sent and summed in bfloat16 or wider, within the bound.
No kernel may reach another device: no remote copies, remote signals or barrier semaphores. Data moves between devices by JAX's collectives and lax.ppermute only.
A program may use at most 32 MiB of HBM per device.

```python
import jax
import jax.numpy as jnp
from jax import lax

D = 5120
KVW = 512
TOKENS = 81920
N_REPLICA = 64


def draw_exponents(key, part):
    bit_count = N_REPLICA.bit_length() - 1
    top_bit = jnp.int32(bit_count - 1)
    other_bit = jax.random.randint(jax.random.fold_in(key, 11), (), 0, bit_count - 1).astype(jnp.int32)
    order_flag = jax.random.randint(jax.random.fold_in(key, 12), (), 0, 2).astype(jnp.int32)
    first_bit = jnp.where(order_flag == 0, top_bit, other_bit)
    second_bit = jnp.where(order_flag == 0, other_bit, top_bit)
    return jnp.stack([first_bit, second_bit]).astype(jnp.int32)


def block_scale(stream_key, extent, pieces, smallest, largest):
    gain, own = 1.0, jax.random.fold_in(stream_key, 6)
    for dim, blocks in pieces:
        draws = jnp.exp(jax.random.uniform(jax.random.fold_in(own, dim), (blocks,), jnp.float32, smallest / len(pieces), largest / len(pieces)))
        gain = gain * jnp.repeat(draws, extent[dim] // blocks).reshape([-1 if axis == dim else 1 for axis in range(len(extent))])
    return gain


def gaussian(key, dims, scale, limit, cuts=(), kind=jnp.bfloat16):
    drawn = scale * jax.random.normal(key, dims, jnp.float32)
    if cuts:
        drawn = drawn * block_scale(key, dims, cuts, -0.22, 0.18)
    return jnp.clip(drawn, -limit, limit).astype(kind)


def setup_inputs(seed: int = 0) -> dict:
    streams_of = jax.random.split(jax.random.key(seed), 5)
    return {
        "features": gaussian(streams_of[0], (TOKENS, D), 1.0, 6.0, ((0, 64), (1, 16))),
        "key_grad": gaussian(streams_of[1], (TOKENS, KVW), 0.0442, 0.29882812, ((0, 1024),)),
        "master": gaussian(streams_of[2], (N_REPLICA, D, KVW), 1.0, 6.0, ((0, 64), (1, 16)), jnp.float32),
        "exponents": draw_exponents(jax.random.fold_in(streams_of[4], 71), 0),
    }


step_rate = 0.2


def replica_step(triple):
    features_r, key_grad_r, master_r = triple
    weight_grad = jnp.dot(features_r.T, key_grad_r, preferred_element_type=jnp.float32)
    working = master_r.astype(jnp.bfloat16)
    input_rows = jnp.dot(key_grad_r, working.T, preferred_element_type=jnp.float32).astype(jnp.bfloat16)
    stepped = master_r - step_rate * weight_grad
    return stepped, input_rows


def reference(features, key_grad, master, exponents):
    groups = master.shape[0]
    grouped_feat = features.reshape(groups, -1, features.shape[1])
    grouped_grad = key_grad.reshape(groups, -1, key_grad.shape[1])
    stepped, input_rows = lax.map(replica_step, (grouped_feat, grouped_grad, master))
    indices = jnp.arange(groups, dtype=jnp.int32)
    for which_round in range(2):
        partner = jnp.bitwise_xor(indices, jnp.left_shift(jnp.int32(1), exponents[which_round].astype(jnp.int32)))
        stepped = 0.5 * (stepped + jnp.take(stepped, partner, axis=0))
    return stepped, stepped.astype(jnp.bfloat16), input_rows.reshape(-1, features.shape[1])
```

```python
from functools import partial

import jax
import jax.numpy as jnp
from jax import lax
from jax.sharding import Mesh
from jax.sharding import PartitionSpec as P

step_rate = 0.2
BITS = ("r5", "r4", "r3", "r2", "r1", "r0")


def spread(block, axes, count):
    copies = jnp.broadcast_to(block[None], (count,) + block.shape)
    return lax.all_to_all(copies, axes, split_axis=0, concat_axis=0, tiled=True)


def swap(values, axis):
    return lax.ppermute(values, axis, [(0, 1), (1, 0)])


def swap_low(low_bit, values):
    return lax.switch(low_bit, [partial(swap, axis=BITS[5 - bit]) for bit in range(5)], values)


def shift(values, step):
    return lax.ppermute(values, "y", [(i, (i + step) % 8) for i in range(8)])


def gather_ring(block):
    me = lax.axis_index("y")
    right_x = lax.axis_index("x") == 1
    other = swap(block, "x")
    both = jnp.concatenate([jnp.where(right_x, other, block), jnp.where(right_x, block, other)], axis=0)
    rows = both.shape[0]
    whole = jnp.zeros((8 * rows, both.shape[1]), both.dtype)

    def put(whole, piece, source, offset=0):
        return lax.dynamic_update_slice(whole, piece, ((source % 8) * rows + offset, 0))

    whole = put(whole, both, me)
    up = down = both
    for step in range(1, 4):
        up, down = shift(up, 1), shift(down, -1)
        whole = put(put(whole, up, me - step), down, me + step)
    cut = rows // 2
    whole = put(whole, shift(up[:cut], 1), me + 4)
    return put(whole, shift(down[cut:], -1), me + 4, cut)


def local(features, key_grad, master, exponents):
    shard = master[0]
    working = shard.astype(jnp.bfloat16)
    block_rows = gather_ring(key_grad)
    weight_grad = lax.dot_general(
        features, block_rows, (((0,), (0,)), ((), ())), preferred_element_type=jnp.float32
    )
    stepped = shard - step_rate * weight_grad
    low_bit = jnp.minimum(exponents[0], exponents[1])
    upper = (lax.axis_index(BITS) >> low_bit) & 1 == 1
    half = stepped.shape[0] // 2
    top, bottom = stepped[:half], stepped[half:]
    given = jnp.where(upper, top, bottom).astype(jnp.bfloat16)
    kept = jnp.where(upper, bottom, top)
    pair = kept + swap_low(low_bit, given).astype(jnp.float32)
    other_pair = swap(pair.astype(jnp.bfloat16), "r5")
    mine = 0.25 * (pair + other_pair.astype(jnp.float32))
    rest = swap_low(low_bit, mine.astype(jnp.bfloat16)).astype(jnp.float32)
    mixed = jnp.concatenate([jnp.where(upper, rest, mine), jnp.where(upper, mine, rest)], axis=0)
    input_rows = lax.dot_general(
        block_rows, working, (((1,), (1,)), ((), ())), preferred_element_type=jnp.float32
    )
    return (mixed[None], mixed.astype(jnp.bfloat16)[None], input_rows.astype(jnp.bfloat16))


def solution(mesh):
    fine = Mesh(mesh.devices.reshape((2,) * 6 + (8, 2)), BITS + ("y", "x"))
    in_specs = (
        P(BITS, ("y", "x")),
        P(BITS + ("y", "x"), None),
        P(BITS, ("y", "x"), None),
        P(),
    )
    out_specs = (P(BITS, ("y", "x"), None), P(BITS, ("y", "x"), None), P(BITS, ("y", "x")))
    return jax.shard_map(local, mesh=fine, in_specs=in_specs, out_specs=out_specs, check_vma=False)
```

```python
from functools import partial

import jax
import jax.numpy as jnp
from jax import lax
from jax.sharding import Mesh
from jax.sharding import PartitionSpec as P

step_rate = 0.2
BITS = ("r5", "r4", "r3", "r2", "r1", "r0")


def swap(values, axis):
    return lax.ppermute(values, axis, [(0, 1), (1, 0)])


EVEN = [(y, y ^ 1) for y in range(8)]
ODD = [(y, (((y + 1) ^ 1) - 1) % 8) for y in range(8)]


def gather(block, low_bit):
    rows, width = block.shape
    y, x = lax.axis_index("y"), lax.axis_index("x")
    ahead = jnp.where(y % 2 == 0, 1, -1)
    whole = jnp.zeros((16 * rows, width), block.dtype)

    def put(whole, pieces, side, sources):
        for number, source in enumerate(sources):
            piece = pieces[number * rows : (number + 1) * rows]
            whole = lax.dynamic_update_slice(whole, piece, (((source % 8) * 2 + side) * rows, 0))
        return whole

    near = jnp.where(y < 8, block, jnp.zeros_like(block))
    near, far, low_bit = lax.optimization_barrier((near, swap(block, "x"), low_bit))
    lanes = [(near, x, (EVEN, ODD), ahead), (far, 1 - x, (ODD, EVEN), -ahead)]
    for own, side, (first, second), d in lanes:
        one = lax.ppermute(own, "y", first)
        two = lax.ppermute(jnp.concatenate([own, one], axis=0), "y", second)
        three = lax.ppermute(two, "y", first)
        four = lax.ppermute(three, "y", second)
        whole = put(whole, own, side, [y])
        whole = put(whole, one, side, [y + d])
        whole = put(whole, two, side, [y - d, y - 2 * d])
        whole = put(whole, three, side, [y + 2 * d, y + 3 * d])
        whole = put(whole, four, side, [y - 3 * d, y - 4 * d])
    return whole, low_bit


def finish(shard, weight_grad, block_rows, low):
    stepped = shard - step_rate * weight_grad
    upper = lax.axis_index(low) == 1
    half = stepped.shape[0] // 2
    top, bottom = stepped[:half], stepped[half:]
    given = jnp.where(upper, top, bottom).astype(jnp.bfloat16)
    kept = lax.optimization_barrier(jnp.where(upper, bottom, top))
    pair = lax.optimization_barrier(kept + swap(given, low).astype(jnp.float32))
    other_pair = swap(pair.astype(jnp.bfloat16), "r5")
    input_rows = lax.dot_general(
        block_rows,
        shard.astype(jnp.bfloat16),
        (((1,), (1,)), ((), ())),
        preferred_element_type=jnp.float32,
    )
    other_pair, input_rows = lax.optimization_barrier((other_pair, input_rows.astype(jnp.bfloat16)))
    mine = 0.25 * (pair + other_pair.astype(jnp.float32))
    rest = swap(mine.astype(jnp.bfloat16), low).astype(jnp.float32)
    is_mine = (lax.broadcasted_iota(jnp.int32, (2, 1, 1), 0) == 1) == upper
    mixed = jnp.where(is_mine, mine[None], rest[None]).reshape(stepped.shape)
    return mixed[None], mixed.astype(jnp.bfloat16)[None], input_rows


def local(features, key_grad, master, exponents):
    shard = master[0]
    low_bit = jnp.minimum(exponents[0], exponents[1])
    block_rows, low_bit = gather(key_grad, low_bit)
    weight_grad = lax.dot_general(
        features, block_rows, (((0,), (0,)), ((), ())), preferred_element_type=jnp.float32
    )
    tails = [partial(finish, low=BITS[5 - bit]) for bit in range(5)]
    return lax.switch(low_bit, tails, shard, weight_grad, block_rows)


def solution(mesh):
    fine = Mesh(mesh.devices.reshape((2,) * 6 + (8, 2)), BITS + ("y", "x"))
    in_specs = (
        P(BITS, ("y", "x")),
        P(BITS + ("y", "x"), None),
        P(BITS, ("y", "x"), None),
        P(),
    )
    out_specs = (P(BITS, ("y", "x"), None), P(BITS, ("y", "x"), None), P(BITS, ("y", "x")))
    return jax.shard_map(local, mesh=fine, in_specs=in_specs, out_specs=out_specs, check_vma=False)
```

```python
from functools import partial

import jax
import jax.numpy as jnp
from jax import lax
from jax.sharding import Mesh
from jax.sharding import PartitionSpec as P

step_rate = 0.2
BITS = ("r5", "r4", "r3", "r2", "r1", "r0")


def swap(values, axis):
    return lax.ppermute(values, axis, [(0, 1), (1, 0)])


EVEN = [(y, y ^ 1) for y in range(8)]
ODD = [(y, (((y + 1) ^ 1) - 1) % 8) for y in range(8)]


def gather(block, low_bit):
    rows, width = block.shape
    y, x = lax.axis_index("y"), lax.axis_index("x")
    ahead = jnp.where(y % 2 == 0, 1, -1)
    whole = jnp.zeros((16 * rows, width), block.dtype)

    def put(whole, pieces, side, sources):
        for number, source in enumerate(sources):
            piece = pieces[number * rows : (number + 1) * rows]
            whole = lax.dynamic_update_slice(whole, piece, (((source % 8) * 2 + side) * rows, 0))
        return whole

    near = jnp.where(y < 8, block, jnp.zeros_like(block))
    near, far, low_bit = lax.optimization_barrier((near, swap(block, "x"), low_bit))
    lanes = [(near, x, (EVEN, ODD), ahead), (far, 1 - x, (ODD, EVEN), -ahead)]
    for own, side, (first, second), d in lanes:
        one = lax.ppermute(own, "y", first)
        two = lax.ppermute(jnp.concatenate([own, one], axis=0), "y", second)
        three = lax.ppermute(two, "y", first)
        four = lax.ppermute(three, "y", second)
        whole = put(whole, own, side, [y])
        whole = put(whole, one, side, [y + d])
        whole = put(whole, two, side, [y - d, y - 2 * d])
        whole = put(whole, three, side, [y + 2 * d, y + 3 * d])
        whole = put(whole, four, side, [y - 3 * d, y - 4 * d])
    return whole, low_bit


def finish(shard, weight_grad, block_rows, low):
    stepped = shard - step_rate * weight_grad
    upper = lax.axis_index(low) == 1
    half = stepped.shape[0] // 2
    top, bottom = stepped[:half], stepped[half:]
    given = jnp.where(upper, top, bottom).astype(jnp.bfloat16)
    kept = lax.optimization_barrier(jnp.where(upper, bottom, top))
    pair = lax.optimization_barrier(kept + swap(given, low).astype(jnp.float32))
    other_pair = swap(pair.astype(jnp.bfloat16), "r5")
    input_rows = lax.dot_general(
        block_rows,
        shard.astype(jnp.bfloat16),
        (((1,), (1,)), ((), ())),
        preferred_element_type=jnp.float32,
    )
    other_pair, input_rows = lax.optimization_barrier((other_pair, input_rows.astype(jnp.bfloat16)))
    mine = 0.25 * (pair + other_pair.astype(jnp.float32))
    rest = swap(mine.astype(jnp.bfloat16), low).astype(jnp.float32)
    is_mine = (lax.broadcasted_iota(jnp.int32, (2, 1, 1), 0) == 1) == upper
    mixed = jnp.where(is_mine, mine[None], rest[None]).reshape(stepped.shape)
    return mixed[None], mixed.astype(jnp.bfloat16)[None], input_rows


def finish_four(shard, weight_grad, block_rows, low):
    stepped = shard - step_rate * weight_grad
    rows, width = stepped.shape
    axes = ("r5", low)
    input_rows = lax.dot_general(
        block_rows,
        shard.astype(jnp.bfloat16),
        (((1,), (1,)), ((), ())),
        preferred_element_type=jnp.float32,
    ).astype(jnp.bfloat16)
    pieces = stepped.astype(jnp.bfloat16).reshape(4, rows // 4, width)
    arrived = lax.all_to_all(pieces, axes, split_axis=0, concat_axis=0, tiled=True)
    arrived, input_rows = lax.optimization_barrier((arrived, input_rows))
    mine = 0.25 * jnp.sum(arrived.astype(jnp.float32), axis=0)
    copies = jnp.broadcast_to(mine.astype(jnp.bfloat16)[None], pieces.shape)
    back = lax.all_to_all(copies, axes, split_axis=0, concat_axis=0, tiled=True)
    is_mine = lax.broadcasted_iota(jnp.int32, (4, 1, 1), 0) == lax.axis_index(axes)
    mixed = jnp.where(is_mine, mine[None], back.astype(jnp.float32)).reshape(stepped.shape)
    return mixed[None], mixed.astype(jnp.bfloat16)[None], input_rows


def local(features, key_grad, master, exponents):
    shard = master[0]
    low_bit = jnp.minimum(exponents[0], exponents[1])
    block_rows, low_bit = gather(key_grad, low_bit)
    weight_grad = lax.dot_general(
        features, block_rows, (((0,), (0,)), ((), ())), preferred_element_type=jnp.float32
    )
    forms = (finish, finish, finish, finish, finish_four)
    tails = [partial(form, low=BITS[5 - bit]) for bit, form in enumerate(forms)]
    return lax.switch(low_bit, tails, shard, weight_grad, block_rows)


def solution(mesh):
    fine = Mesh(mesh.devices.reshape((2,) * 6 + (8, 2)), BITS + ("y", "x"))
    in_specs = (
        P(BITS, ("y", "x")),
        P(BITS + ("y", "x"), None),
        P(BITS, ("y", "x"), None),
        P(),
    )
    out_specs = (P(BITS, ("y", "x"), None), P(BITS, ("y", "x"), None), P(BITS, ("y", "x")))
    return jax.shard_map(local, mesh=fine, in_specs=in_specs, out_specs=out_specs, check_vma=False)
```
